32 devices in a mesh: win: 16 (over z, y, core), chan: 2 (over x).
Axes of the slice: x: 2, y: 2, z: 4, core: 2. Of those that a mesh axis runs over, the one named last changes fastest.
Arguments:
- traces: bfloat16 [32, 512, 4096], P('win', 'chan'), may hold values from -120 to 120
- block_pairs: int32 [16, 2], replicated, may hold values from 0 to 3
- valid_count: int32 [1], replicated, may hold values from 4 to 15
Outputs:
- cross_spectra: float32 [16, 8, 2, 128, 128], P('win', 'chan')
The draws below stay inside these ranges and needn't reach their ends.
Inputs may be any that keep to these rules, and one draw needn't show every extreme that they name: `block_pairs`: entries are channel block numbers; a pair may repeat.
All inputs are finite; a program needn't handle non-finite values.
Results may differ from the reference program's by a relative error of at most 0.0037.
Values may be sent and summed in bfloat16 or wider, within the bound.
A program may use at most 64 MiB of HBM per device.

```python
import math
import jax
import jax.numpy as jnp
from jax import lax

NT = 4096
BLOCK = 128
NBINS = 256
FREQ_LO = 64
GROUP = 32
WINDOWS = 32
CH = 512
NB = 4
NP = 16
GROUPS = 8


def draw_traces(key, part):
    keys = jax.random.split(jax.random.fold_in(key, 7), 5)
    noise = jnp.clip(jax.random.normal(keys[0], (WINDOWS, CH, NT), jnp.float32), -6.0, 6.0)
    gain = jnp.exp(jax.random.uniform(keys[1], (1, CH, 1), jnp.float32, 0.0, math.log(10.0)))
    tone_bin = FREQ_LO + jax.random.randint(keys[2], (1, CH, 1), 0, NBINS)
    amplitude = jnp.exp(jax.random.uniform(keys[3], (1, CH, 1), jnp.float32, math.log(0.1), math.log(0.5)))
    phase = jax.random.uniform(keys[4], (WINDOWS, CH, 1), jnp.float32, -math.pi, math.pi)
    times = jnp.arange(NT, dtype=jnp.int32)[None, None, :]
    turns = times * tone_bin % NT
    tone = amplitude * jnp.cos(turns.astype(jnp.float32) * (2.0 * math.pi / NT) + phase)
    return (gain * (noise + tone)).astype(jnp.bfloat16)


def with_ends(entries, key, least, high):
    dims = entries.shape
    spot = [jax.random.randint(jax.random.fold_in(key, axis), (), 0, dims[axis]) for axis in range(len(dims))]
    entries = entries.at[tuple(spot)].set(least)
    longest = dims.index(max(dims))
    spot[longest] = (spot[longest] + 1) % dims[longest]
    return entries.at[tuple(spot)].set(high)


def setup_inputs(seed: int = 0) -> dict:
    seeds = jax.random.split(jax.random.key(seed), 4)
    return {
        "traces": draw_traces(jax.random.fold_in(seeds[3], 71), 0),
        "block_pairs": with_ends(jax.random.randint(seeds[1], (NP, 2), 0, NB), jax.random.fold_in(seeds[1], 1), 0, NB - 1).astype(jnp.int32),
        "valid_count": jax.random.randint(seeds[2], (1,), NP // 4, NP).astype(jnp.int32),
    }


def dft_table(length, first_bin, bins):
    times = jnp.arange(length, dtype=jnp.int32)
    freqs = first_bin + jnp.arange(bins, dtype=jnp.int32)
    phases = times[:, None] * freqs[None, :] % length
    angles = phases.astype(jnp.float32) * (2.0 * math.pi / length)
    factor = 1.0 / math.sqrt(length)
    return (jnp.concatenate([jnp.cos(angles), -jnp.sin(angles)], axis=1) * factor).astype(jnp.bfloat16)

def reference(traces, block_pairs, valid_count):
    table = dft_table(NT, FREQ_LO, NBINS)

    def whiten(window_traces):
        spectra = jnp.dot(window_traces, table, preferred_element_type=jnp.float32)
        energy = lax.optimization_barrier(jnp.sum(spectra * spectra, axis=1, keepdims=True)) / NBINS
        return (spectra * lax.rsqrt(energy + 1e-06)).astype(jnp.bfloat16)
    whitened = lax.map(whiten, traces)
    real_part = whitened[:, :, :NBINS].astype(jnp.float32).reshape(WINDOWS, CH, GROUPS, GROUP)
    imag_part = whitened[:, :, NBINS:].astype(jnp.float32).reshape(WINDOWS, CH, GROUPS, GROUP)
    stack_scale = 1.0 / math.sqrt(WINDOWS * GROUP)
    high = lax.Precision.HIGHEST

    def one_slot(slot):
        row_start = (block_pairs[slot, 0] * BLOCK).astype(jnp.int32)
        col_start = (block_pairs[slot, 1] * BLOCK).astype(jnp.int32)
        a_re = lax.dynamic_slice_in_dim(real_part, row_start, BLOCK, 1)
        a_im = lax.dynamic_slice_in_dim(imag_part, row_start, BLOCK, 1)
        b_re = lax.dynamic_slice_in_dim(real_part, col_start, BLOCK, 1)
        b_im = lax.dynamic_slice_in_dim(imag_part, col_start, BLOCK, 1)
        sum_re = jnp.einsum('wigf,wjgf->gij', a_re, b_re, precision=high) + jnp.einsum('wigf,wjgf->gij', a_im, b_im, precision=high)
        sum_im = jnp.einsum('wigf,wjgf->gij', a_im, b_re, precision=high) - jnp.einsum('wigf,wjgf->gij', a_re, b_im, precision=high)
        live = (slot < valid_count[0]).astype(jnp.float32)
        return jnp.stack([sum_re, sum_im], axis=1) * (stack_scale * live)
    return lax.map(one_slot, jnp.arange(NP, dtype=jnp.int32))
```

```python
import functools
import math

import jax
import jax.numpy as jnp
import ml_dtypes
import numpy as np
from jax import lax
from jax.experimental import pallas as pl
from jax.experimental.pallas import tpu as pltpu
from jax.sharding import PartitionSpec as P

BLOCK = 128
NBINS = 256
FREQ_LO = 64
GROUP = 32
GROUPS = NBINS // GROUP
EPS = 1e-06
MESH = pl.DeviceIdType.MESH
KCH = 4


def dft_table(length):
    times = np.arange(length, dtype=np.int32)
    freqs = FREQ_LO + np.arange(NBINS, dtype=np.int32)
    phases = times[:, None] * freqs[None, :] % length
    angles = phases.astype(np.float32) * np.float32(2.0 * math.pi / length)
    wide = angles.astype(np.float64)
    factor = np.float32(1.0 / math.sqrt(length))
    re = np.cos(wide).astype(np.float32) * factor
    im = -np.sin(wide).astype(np.float32) * factor
    table = np.stack(
        [re.reshape(length, GROUPS, GROUP), im.reshape(length, GROUPS, GROUP)], axis=2
    )
    return table.reshape(length, 2 * NBINS).astype(ml_dtypes.bfloat16)


def kernel(
    dims, tr_hbm, table_hbm, pairs, out,
    tr, table, acc, send, held, turned, outbox, inbox, relay, mail, done,
    in_sem, self_sem, a_send, a_recv, p_send, p_recv, r_recv, f_send, f_recv,
):
    planes, sub, chans, spp, spd, chl, length, relayed = dims
    win, x = lax.axis_index("win"), lax.axis_index("chan")
    q, j = win // sub, win % sub
    g = x * sub + j
    kc = length // KCH
    nch = chl // BLOCK

    def tr_copy(c, k):
        part = (slice(None), pl.ds(c * BLOCK, BLOCK), pl.ds(k * kc, kc))
        return pltpu.make_async_copy(tr_hbm.at[part], tr.at[part], in_sem.at[c * KCH + k])

    def table_copy(k):
        part = pl.ds(k * kc, kc)
        return pltpu.make_async_copy(table_hbm.at[part], table.at[part], in_sem.at[nch * KCH + k])

    for k in range(KCH):
        tr_copy(0, k).start()
        table_copy(k).start()
    for c in range(1, nch):
        for k in range(KCH):
            tr_copy(c, k).start()

    barrier = pltpu.get_barrier_semaphore()

    @pl.loop(1, GROUPS)
    def _(o):
        to = (g + o) % GROUPS
        pl.semaphore_signal(
            barrier, inc=1, device_id=(q * sub + to % sub, to // sub), device_id_type=MESH
        )

    @pl.loop(1, planes)
    def _(o):
        pl.semaphore_signal(
            barrier, inc=1, device_id=(((q + o) % planes) * sub + j, x), device_id_type=MESH
        )

    def a_copy(c, o, to):
        return pltpu.make_async_remote_copy(
            src_ref=send.at[to, pl.ds(c * BLOCK, BLOCK), :],
            dst_ref=held.at[j, x * nch + c],
            send_sem=a_send.at[c, o],
            recv_sem=a_recv.at[c, o],
            device_id=(q * sub + to % sub, to // sub),
            device_id_type=MESH,
        )

    low = lax.broadcasted_iota(jnp.int32, (BLOCK, 128), 1) < 2 * GROUP
    for c in range(nch):
        for k in range(KCH):
            tr_copy(c, k).wait()
            if c == 0:
                table_copy(k).wait()
            rows = tr[:, c * BLOCK : (c + 1) * BLOCK, k * kc : (k + 1) * kc]
            term = jnp.dot(
                rows.reshape(2 * BLOCK, kc),
                table[k * kc : (k + 1) * kc, :],
                preferred_element_type=jnp.float32,
            )
            if k == 0:
                acc[...] = term
            else:
                acc[...] += term
        spectra = acc[...]
        energy = jnp.sum(spectra * spectra, axis=1, keepdims=True) / NBINS
        white = spectra * lax.rsqrt(energy + EPS)
        for h in range(GROUPS // 2):
            a = white[:BLOCK, h * 128 : (h + 1) * 128]
            b = white[BLOCK:, h * 128 : (h + 1) * 128]
            even = jnp.where(low, a, pltpu.roll(b, 64, 1))
            odd = jnp.where(low, pltpu.roll(a, 64, 1), b)
            send[2 * h, c * BLOCK : (c + 1) * BLOCK, :] = even.astype(jnp.bfloat16)
            send[2 * h + 1, c * BLOCK : (c + 1) * BLOCK, :] = odd.astype(jnp.bfloat16)
        if c == 0:
            pl.semaphore_wait(barrier, GROUPS - 1 + planes - 1)

        @pl.loop(1, GROUPS)
        def _(o):
            a_copy(c, o, (g + o) % GROUPS).start()

        pltpu.make_async_copy(
            send.at[g, pl.ds(c * BLOCK, BLOCK), :],
            held.at[j, x * nch + c],
            self_sem.at[c],
        ).start()

    for c in range(nch):
        pltpu.make_async_copy(
            send.at[g, pl.ds(c * BLOCK, BLOCK), :],
            held.at[j, x * nch + c],
            self_sem.at[c],
        ).wait()

        @pl.loop(1, GROUPS)
        def _(o):
            src = (g + GROUPS - o) % GROUPS
            pltpu.make_async_remote_copy(
                src_ref=send.at[src, pl.ds(c * BLOCK, BLOCK), :],
                dst_ref=held.at[src % sub, (src // sub) * nch + c],
                send_sem=a_send.at[c, o],
                recv_sem=a_recv.at[c, o],
                device_id=(q * sub + src % sub, src // sub),
                device_id_type=MESH,
            ).wait_recv()

    row = lax.broadcasted_iota(jnp.int32, (128, 128), 0)
    col = lax.broadcasted_iota(jnp.int32, (128, 128), 1)
    is_re = col % (2 * GROUP) < GROUP
    turn = jnp.where(
        is_re,
        jnp.where(row == col + GROUP, 1.0, 0.0),
        jnp.where(row + GROUP == col, -1.0, 0.0),
    ).astype(jnp.bfloat16)
    for m in range(sub):

        @pl.loop(0, chans * nch)
        def _(b):
            turned[m, b] = jnp.dot(
                held[m, b], turn, preferred_element_type=jnp.float32
            ).astype(jnp.bfloat16)

    def partial(p):
        r, s = pairs[p, 0], pairs[p, 1]
        upper = jnp.concatenate(
            [
                jnp.concatenate([held[m, r] for m in range(sub)], axis=1),
                jnp.concatenate([turned[m, r] for m in range(sub)], axis=1),
            ],
            axis=0,
        )
        lower = jnp.concatenate([held[m, s] for m in range(sub)], axis=1)
        return lax.dot_general(
            upper, lower, (((1,), (1,)), ((), ())), preferred_element_type=jnp.float32
        )

    first_half = q < planes // 2
    last = planes - 1

    def dest(k):
        return jnp.where(first_half, (q + planes - k) % planes, (q + k) % planes)

    def p_copy(d, i, to):
        return pltpu.make_async_remote_copy(
            src_ref=outbox.at[d, i],
            dst_ref=inbox.at[q, i],
            send_sem=p_send.at[d, i],
            recv_sem=p_recv.at[q, i],
            device_id=(to * sub + j, x),
            device_id_type=MESH,
        )

    def r_copy(d, i, to):
        return pltpu.make_async_remote_copy(
            src_ref=outbox.at[d, i],
            dst_ref=relay.at[i],
            send_sem=p_send.at[d, i],
            recv_sem=r_recv.at[i],
            device_id=(to * sub + j, x),
            device_id_type=MESH,
        )

    far = last - q
    far_relayed = jnp.logical_or(q == 0, q == last)
    relays = jnp.logical_or(q == 1, q == last - 1)
    rdest = jnp.where(q == 1, last, 0)
    rnext = jnp.where(q == 0, 1, last - 1)

    @pl.loop(0, (planes - 1) * spp)
    def _(n):
        d, i = dest(n // spp + 1), n % spp
        t = (j * spd + spd + i) % spp

        def send_out():
            outbox[d, i] = partial(d * spp + t).astype(jnp.bfloat16)

        if not relayed:
            send_out()
            p_copy(d, i, d).start()
        else:
            held_back = jnp.logical_and(relays, d == rdest)

            @pl.when(jnp.logical_not(held_back))
            def _():
                send_out()
                via = jnp.logical_and(far_relayed, d == far)

                @pl.when(via)
                def _():
                    r_copy(d, i, rnext).start()

                @pl.when(jnp.logical_not(via))
                def _():
                    p_copy(d, i, d).start()

    if relayed:

        @pl.when(relays)
        def _():
            @pl.loop(0, spp)
            def _(i):
                t = (j * spd + spd + i) % spp
                value = partial(rdest * spp + t)
                r_copy(rdest, i, rdest).wait_recv()
                outbox[rdest, i] = (value + relay[i].astype(jnp.float32)).astype(jnp.bfloat16)
                p_copy(rdest, i, rdest).start()

    def f_copy(t, owner):
        return pltpu.make_async_remote_copy(
            src_ref=done.at[t],
            dst_ref=mail.at[j, t % spd],
            send_sem=f_send.at[t],
            recv_sem=f_recv.at[j, t % spd],
            device_id=(q * sub + owner, x),
            device_id_type=MESH,
        )

    def through_relay(src):
        return jnp.logical_or(
            jnp.logical_and(q == last, src == 0), jnp.logical_and(q == 0, src == last)
        )

    @pl.loop(0, spp)
    def _(i):
        t = (j * spd + spd + i) % spp
        done[t] = partial(q * spp + t)

    @pl.loop(0, spp)
    def _(i):
        t = (j * spd + spd + i) % spp

        @pl.loop(1, planes)
        def _(o):
            src = (q + o) % planes

            def take():
                pltpu.make_async_remote_copy(
                    src_ref=outbox.at[src, i],
                    dst_ref=inbox.at[src, i],
                    send_sem=p_send.at[src, i],
                    recv_sem=p_recv.at[src, i],
                    device_id=(src * sub + j, x),
                    device_id_type=MESH,
                ).wait_recv()
                done[t] += inbox[src, i].astype(jnp.float32)

            if relayed:
                pl.when(jnp.logical_not(through_relay(src)))(take)
            else:
                take()

        @pl.when(t // spd != j)
        def _():
            f_copy(t, t // spd).start()

        @pl.when(t // spd == j)
        def _():
            out[t % spd, j] = done[t]

    for m in range(1, sub):
        src = (j + m) % sub
        for e in range(spd):
            pltpu.make_async_remote_copy(
                src_ref=done.at[e],
                dst_ref=mail.at[src, e],
                send_sem=f_send.at[e],
                recv_sem=f_recv.at[src, e],
                device_id=(q * sub + src, x),
                device_id_type=MESH,
            ).wait_recv()
            out[e, src] = mail[src, e]

    for c in range(nch):

        @pl.loop(1, GROUPS)
        def _(o):
            a_copy(c, o, (g + o) % GROUPS).wait_send()

    @pl.loop(0, (planes - 1) * spp)
    def _(n):
        d, i = dest(n // spp + 1), n % spp
        p_copy(d, i, d).wait_send()

    @pl.loop(0, spp)
    def _(t):
        @pl.when(t // spd != j)
        def _():
            f_copy(t, t // spd).wait_send()


def on_device(planes, sub, chans, table, traces, block_pairs, valid_count):
    windows, chl, length = traces.shape
    slots = block_pairs.shape[0]
    spp, spd = slots // planes, slots // (planes * sub)
    relayed = planes >= 4
    dims = (planes, sub, chans, spp, spd, chl, length, relayed)
    bf, f32 = jnp.bfloat16, jnp.float32
    nch = chl // BLOCK
    sums = pl.pallas_call(
        functools.partial(kernel, dims),
        name="cross_spectra",
        out_shape=jax.ShapeDtypeStruct((spd, sub, 2 * BLOCK, BLOCK), f32),
        in_specs=[
            pl.BlockSpec(memory_space=pl.ANY),
            pl.BlockSpec(memory_space=pl.ANY),
            pl.BlockSpec(memory_space=pltpu.SMEM),
        ],
        out_specs=pl.BlockSpec(memory_space=pltpu.VMEM),
        scratch_shapes=[
            pltpu.VMEM((windows, chl, length), bf),
            pltpu.VMEM((length, 2 * NBINS), bf),
            pltpu.VMEM((windows * BLOCK, 2 * NBINS), f32),
            pltpu.VMEM((GROUPS, chl, 128), bf),
            pltpu.VMEM((sub, chans * nch, BLOCK, 128), bf),
            pltpu.VMEM((sub, chans * nch, BLOCK, 128), bf),
            pltpu.VMEM((planes, spp, 2 * BLOCK, BLOCK), bf),
            pltpu.VMEM((planes, spp, 2 * BLOCK, BLOCK), bf),
            pltpu.VMEM((spp, 2 * BLOCK, BLOCK), bf),
            pltpu.VMEM((sub, spd, 2 * BLOCK, BLOCK), f32),
            pltpu.VMEM((spp, 2 * BLOCK, BLOCK), f32),
            pltpu.SemaphoreType.DMA(((nch + 1) * KCH,)),
            pltpu.SemaphoreType.DMA((nch,)),
            pltpu.SemaphoreType.DMA((nch, GROUPS)),
            pltpu.SemaphoreType.DMA((nch, GROUPS)),
            pltpu.SemaphoreType.DMA((planes, spp)),
            pltpu.SemaphoreType.DMA((planes, spp)),
            pltpu.SemaphoreType.DMA((spp,)),
            pltpu.SemaphoreType.DMA((spp,)),
            pltpu.SemaphoreType.DMA((sub, spd)),
        ],
        compiler_params=pltpu.CompilerParams(
            collective_id=0, has_side_effects=True, vmem_limit_bytes=60 * 1024 * 1024
        ),
        cost_estimate=pl.CostEstimate(
            flops=2 * windows * chl * length * 2 * NBINS,
            bytes_accessed=2 * (windows * chl * length + length * 2 * NBINS),
            transcendentals=0,
        ),
    )(traces, table, block_pairs)
    stack_scale = 1.0 / math.sqrt(windows * planes * sub * GROUP)
    slot_ids = lax.axis_index("win") * spd + jnp.arange(spd, dtype=jnp.int32)
    live = (slot_ids < valid_count[0]).astype(f32)
    sums = sums.reshape(spd, sub, 2, BLOCK, BLOCK)
    return sums * (stack_scale * live)[:, None, None, None, None]


def solution(mesh):
    wins, chans = mesh.shape["win"], mesh.shape["chan"]
    sub = GROUPS // chans
    planes = wins // sub

    def run(traces, block_pairs, valid_count):
        table = jnp.asarray(dft_table(traces.shape[2]))
        body = functools.partial(on_device, planes, sub, chans)
        return jax.shard_map(
            body,
            mesh=mesh,
            in_specs=(P(), P("win", "chan", None), P(), P()),
            out_specs=P("win", "chan", None, None, None),
            check_vma=False,
        )(table, traces, block_pairs, valid_count)

    return run
```

```python
import functools
import math

import jax
import jax.numpy as jnp
import ml_dtypes
import numpy as np
from jax import lax
from jax.experimental import pallas as pl
from jax.experimental.pallas import tpu as pltpu
from jax.sharding import PartitionSpec as P

BLOCK = 128
NBINS = 256
FREQ_LO = 64
GROUP = 32
GROUPS = NBINS // GROUP
EPS = 1e-06
MESH = pl.DeviceIdType.MESH
KCH = 4


def dft_table(length):
    times = np.arange(length, dtype=np.int32)
    freqs = FREQ_LO + np.arange(NBINS, dtype=np.int32)
    phases = times[:, None] * freqs[None, :] % length
    angles = phases.astype(np.float32) * np.float32(2.0 * math.pi / length)
    wide = angles.astype(np.float64)
    factor = np.float32(1.0 / math.sqrt(length))
    re = np.cos(wide).astype(np.float32) * factor
    im = -np.sin(wide).astype(np.float32) * factor
    table = np.stack(
        [re.reshape(length, GROUPS, GROUP), im.reshape(length, GROUPS, GROUP)], axis=2
    )
    return table.reshape(length, 2 * NBINS).astype(ml_dtypes.bfloat16)


def kernel(
    dims, tr_hbm, table_hbm, pairs, out,
    tr, table, acc, send, held, turned, held2, turned2, outbox, inbox, relay, value,
    in_sem, self_sem, a_send, a_recv, h_send, h_recv, p_send, p_recv, r_recv,
):
    planes, sub, chans, spp, spd, chl, length, relayed, forwards = dims
    win, x = lax.axis_index("win"), lax.axis_index("chan")
    q, j = win // sub, win % sub
    g = x * sub + j
    kc = length // KCH
    nch = chl // BLOCK
    both = jnp.logical_and
    last = planes - 1
    end = jnp.logical_or(q == 0, q == last)
    inner = jnp.logical_or(q == 1, q == last - 1)
    partner = jnp.where(q == 0, 1, jnp.where(q == 1, 0, jnp.where(q == last, last - 1, last)))
    by_data = (j % 2 == 0) if forwards else (j < 0)

    def tr_copy(c, k):
        part = (slice(None), pl.ds(c * BLOCK, BLOCK), pl.ds(k * kc, kc))
        return pltpu.make_async_copy(tr_hbm.at[part], tr.at[part], in_sem.at[c * KCH + k])

    def table_copy(k):
        part = pl.ds(k * kc, kc)
        return pltpu.make_async_copy(table_hbm.at[part], table.at[part], in_sem.at[nch * KCH + k])

    for k in range(KCH):
        tr_copy(0, k).start()
        table_copy(k).start()
    for c in range(1, nch):
        for k in range(KCH):
            tr_copy(c, k).start()

    barrier = pltpu.get_barrier_semaphore()

    @pl.loop(sub, GROUPS)
    def _(o):
        to = ((x * sub) + o) % GROUPS
        pl.semaphore_signal(
            barrier, inc=1, device_id=(q * sub + to % sub, to // sub), device_id_type=MESH
        )

    @pl.loop(1, planes * sub)
    def _(o):
        pl.semaphore_signal(
            barrier, inc=1, device_id=((win + o) % (planes * sub), x), device_id_type=MESH
        )

    def a_copy(c, o, to):
        return pltpu.make_async_remote_copy(
            src_ref=send.at[to, pl.ds(c * BLOCK, BLOCK), :],
            dst_ref=held.at[j, x * nch + c],
            send_sem=a_send.at[c, o],
            recv_sem=a_recv.at[c, o],
            device_id=(q * sub + to % sub, to // sub),
            device_id_type=MESH,
        )

    def h_copy(c, src):
        b = (src // sub) * nch + c
        return pltpu.make_async_remote_copy(
            src_ref=held.at[src % sub, b],
            dst_ref=held2.at[src % sub, b],
            send_sem=h_send.at[c, src],
            recv_sem=h_recv.at[c, src],
            device_id=(partner * sub + j, x),
            device_id_type=MESH,
        )

    def forward(c, src):
        if forwards:

            @pl.when(both(end, by_data))
            def _():
                h_copy(c, src).start()

    low = lax.broadcasted_iota(jnp.int32, (BLOCK, 128), 1) < 2 * GROUP
    for c in range(nch):
        for k in range(KCH):
            tr_copy(c, k).wait()
            if c == 0:
                table_copy(k).wait()
            rows = tr[:, c * BLOCK : (c + 1) * BLOCK, k * kc : (k + 1) * kc]
            term = jnp.dot(
                rows.reshape(2 * BLOCK, kc),
                table[k * kc : (k + 1) * kc, :],
                preferred_element_type=jnp.float32,
            )
            if k == 0:
                acc[...] = term
            else:
                acc[...] += term
        spectra = acc[...]
        energy = jnp.sum(spectra * spectra, axis=1, keepdims=True) / NBINS
        white = spectra * lax.rsqrt(energy + EPS)
        for h in range(GROUPS // 2):
            a = white[:BLOCK, h * 128 : (h + 1) * 128]
            b = white[BLOCK:, h * 128 : (h + 1) * 128]
            even = jnp.where(low, a, pltpu.roll(b, 64, 1))
            odd = jnp.where(low, pltpu.roll(a, 64, 1), b)
            send[2 * h, c * BLOCK : (c + 1) * BLOCK, :] = even.astype(jnp.bfloat16)
            send[2 * h + 1, c * BLOCK : (c + 1) * BLOCK, :] = odd.astype(jnp.bfloat16)
        if c == 0:
            pl.semaphore_wait(barrier, GROUPS - sub + planes * sub - 1)

        @pl.loop(1, GROUPS)
        def _(o):
            a_copy(c, o, (g + o) % GROUPS).start()

        pltpu.make_async_copy(
            send.at[g, pl.ds(c * BLOCK, BLOCK), :],
            held.at[j, x * nch + c],
            self_sem.at[c],
        ).start()

    for c in range(nch):
        pltpu.make_async_copy(
            send.at[g, pl.ds(c * BLOCK, BLOCK), :],
            held.at[j, x * nch + c],
            self_sem.at[c],
        ).wait()
        forward(c, g)

        @pl.loop(1, GROUPS)
        def _(o):
            src = (g + GROUPS - o) % GROUPS
            pltpu.make_async_remote_copy(
                src_ref=send.at[src, pl.ds(c * BLOCK, BLOCK), :],
                dst_ref=held.at[src % sub, (src // sub) * nch + c],
                send_sem=a_send.at[c, o],
                recv_sem=a_recv.at[c, o],
                device_id=(q * sub + src % sub, src // sub),
                device_id_type=MESH,
            ).wait_recv()
            forward(c, src)

    row = lax.broadcasted_iota(jnp.int32, (128, 128), 0)
    col = lax.broadcasted_iota(jnp.int32, (128, 128), 1)
    turn = jnp.where(
        col % (2 * GROUP) < GROUP,
        jnp.where(row == col + GROUP, 1.0, 0.0),
        jnp.where(row + GROUP == col, -1.0, 0.0),
    ).astype(jnp.bfloat16)

    def turn_all(held, turned):
        @pl.loop(0, chans * nch)
        def _(b):
            for m in range(sub):
                turned[m, b] = jnp.dot(
                    held[m, b], turn, preferred_element_type=jnp.float32
                ).astype(jnp.bfloat16)

    turn_all(held, turned)

    def partial(p, held, turned):
        r, s = pairs[0, p], pairs[1, p]
        ms = range(sub)
        upper = jnp.concatenate(
            [
                jnp.concatenate([held[m, r] for m in ms], axis=1),
                jnp.concatenate([turned[m, r] for m in ms], axis=1),
            ],
            axis=0,
        )
        lower = jnp.concatenate([held[m, s] for m in ms], axis=1)
        return lax.dot_general(
            upper, lower, (((1,), (1,)), ((), ())), preferred_element_type=jnp.float32
        )

    def dest(k):
        return jnp.where(q < planes // 2, (q + planes - k) % planes, (q + k) % planes)

    def p_copy(d, i, t):
        return pltpu.make_async_remote_copy(
            src_ref=outbox.at[d, i],
            dst_ref=inbox.at[q, j, t % spd],
            send_sem=p_send.at[d, i],
            recv_sem=p_recv.at[q, j, t % spd],
            device_id=(d * sub + t // spd, x),
            device_id_type=MESH,
        )

    def r_copy(d, i):
        return pltpu.make_async_remote_copy(
            src_ref=outbox.at[d, i],
            dst_ref=relay.at[d, i],
            send_sem=p_send.at[d, i],
            recv_sem=r_recv.at[d, i],
            device_id=(partner * sub + j, x),
            device_id_type=MESH,
        )

    def item(n):
        d, i = dest(n // spp + 1), n % spp
        t = (j * spd + spd + i) % spp
        local = both(d == q, t // spd == j)
        return d, i, t, local

    @pl.loop(0, planes * spp)
    def _(n):
        d, i, t, local = item(n)
        if forwards:

            @pl.when(both(inner, both(by_data, n == spp)))
            def _():
                for c in range(nch):

                    @pl.loop(0, GROUPS)
                    def _(src):
                        h_copy(c, src).wait_recv()

                turn_all(held2, turned2)

        def work():
            value[...] = partial(d * spp + t, held, turned)
            if forwards:

                @pl.when(both(inner, both(by_data, d != partner)))
                def _():
                    value[...] += partial(d * spp + t, held2, turned2)

            if relayed:

                @pl.when(both(both(inner, jnp.logical_not(by_data)), both(d != partner, d != q)))
                def _():
                    r_copy(d, i).wait_recv()
                    value[...] += relay[d, i].astype(jnp.float32)

            @pl.when(local)
            def _():
                out[t % spd, j] = value[...]

            @pl.when(jnp.logical_not(local))
            def _():
                outbox[d, i] = value[...].astype(jnp.bfloat16)
                if relayed:
                    via = both(end, both(d != q, d != partner))

                    @pl.when(via)
                    def _():
                        r_copy(d, i).start()

                    @pl.when(jnp.logical_not(via))
                    def _():
                        p_copy(d, i, t).start()

                else:
                    p_copy(d, i, t).start()

        if forwards:
            pl.when(jnp.logical_not(both(both(end, by_data), d != q)))(work)
        else:
            work()

    def exists(src, m):
        there = jnp.logical_not(both(src == q, m == j))
        if relayed:
            src_end = jnp.logical_or(src == 0, src == last)
            src_partner = jnp.where(src == 0, 1, last - 1)
            direct = src_partner == q
            if forwards:
                direct = both(direct, m % 2 == 1)
            there = both(
                there, jnp.logical_or(src == q, jnp.logical_or(jnp.logical_not(src_end), direct))
            )
        return there

    @pl.loop(0, planes * sub)
    def _(n):
        src, m = (q + n // sub) % planes, n % sub

        @pl.when(exists(src, m))
        def _():
            for e in range(spd):
                pltpu.make_async_remote_copy(
                    src_ref=outbox.at[0, 0],
                    dst_ref=inbox.at[src, m, e],
                    send_sem=p_send.at[0, 0],
                    recv_sem=p_recv.at[src, m, e],
                    device_id=(src * sub + m, x),
                    device_id_type=MESH,
                ).wait_recv()
                got = inbox[src, m, e].astype(jnp.float32)

                @pl.when(both(n < sub, m != j))
                def _():
                    out[e, m] = got

                @pl.when(jnp.logical_not(both(n < sub, m != j)))
                def _():
                    out[e, m] += got

    for c in range(nch):

        @pl.loop(1, GROUPS)
        def _(o):
            a_copy(c, o, (g + o) % GROUPS).wait_send()

        if forwards:

            @pl.when(both(end, by_data))
            def _():
                @pl.loop(0, GROUPS)
                def _(src):
                    h_copy(c, src).wait_send()

    @pl.loop(0, planes * spp)
    def _(n):
        d, i, t, local = item(n)
        sent = jnp.logical_not(local)
        if forwards:
            sent = both(sent, jnp.logical_not(both(both(end, by_data), d != q)))

        @pl.when(sent)
        def _():
            p_copy(d, i, t).wait_send()


def on_device(planes, sub, chans, table, traces, block_pairs, valid_count):
    windows, chl, length = traces.shape
    slots = block_pairs.shape[0]
    spp, spd = slots // planes, slots // (planes * sub)
    relayed = planes >= 4
    dims = (planes, sub, chans, spp, spd, chl, length, relayed, relayed and sub > 1)
    bf, f32 = jnp.bfloat16, jnp.float32
    nch = chl // BLOCK
    sums = pl.pallas_call(
        functools.partial(kernel, dims),
        name="cross_spectra",
        out_shape=jax.ShapeDtypeStruct((spd, sub, 2 * BLOCK, BLOCK), f32),
        in_specs=[
            pl.BlockSpec(memory_space=pl.ANY),
            pl.BlockSpec(memory_space=pl.ANY),
            pl.BlockSpec(memory_space=pltpu.SMEM),
        ],
        out_specs=pl.BlockSpec(memory_space=pltpu.VMEM),
        scratch_shapes=[
            pltpu.VMEM((windows, chl, length), bf),
            pltpu.VMEM((length, 2 * NBINS), bf),
            pltpu.VMEM((windows * BLOCK, 2 * NBINS), f32),
            pltpu.VMEM((GROUPS, chl, 128), bf),
            pltpu.VMEM((sub, chans * nch, BLOCK, 128), bf),
            pltpu.VMEM((sub, chans * nch, BLOCK, 128), bf),
            pltpu.VMEM((sub, chans * nch, BLOCK, 128), bf),
            pltpu.VMEM((sub, chans * nch, BLOCK, 128), bf),
            pltpu.VMEM((planes, spp, 2 * BLOCK, BLOCK), bf),
            pltpu.VMEM((planes, sub, spd, 2 * BLOCK, BLOCK), bf),
            pltpu.VMEM((planes, spp, 2 * BLOCK, BLOCK), bf),
            pltpu.VMEM((2 * BLOCK, BLOCK), f32),
            pltpu.SemaphoreType.DMA(((nch + 1) * KCH,)),
            pltpu.SemaphoreType.DMA((nch,)),
            pltpu.SemaphoreType.DMA((nch, GROUPS)),
            pltpu.SemaphoreType.DMA((nch, GROUPS)),
            pltpu.SemaphoreType.DMA((nch, GROUPS)),
            pltpu.SemaphoreType.DMA((nch, GROUPS)),
            pltpu.SemaphoreType.DMA((planes, spp)),
            pltpu.SemaphoreType.DMA((planes, sub, spd)),
            pltpu.SemaphoreType.DMA((planes, spp)),
        ],
        compiler_params=pltpu.CompilerParams(
            collective_id=0, has_side_effects=True, vmem_limit_bytes=60 * 1024 * 1024
        ),
        cost_estimate=pl.CostEstimate(
            flops=2 * windows * chl * length * 2 * NBINS,
            bytes_accessed=2 * (windows * chl * length + length * 2 * NBINS),
            transcendentals=0,
        ),
    )(traces, table, block_pairs.T)
    stack_scale = 1.0 / math.sqrt(windows * planes * sub * GROUP)
    slot_ids = lax.axis_index("win") * spd + jnp.arange(spd, dtype=jnp.int32)
    live = (slot_ids < valid_count[0]).astype(f32)
    sums = sums.reshape(spd, sub, 2, BLOCK, BLOCK)
    return sums * (stack_scale * live)[:, None, None, None, None]


def solution(mesh):
    wins, chans = mesh.shape["win"], mesh.shape["chan"]
    sub = GROUPS // chans
    planes = wins // sub

    def run(traces, block_pairs, valid_count):
        table = jnp.asarray(dft_table(traces.shape[2]))
        body = functools.partial(on_device, planes, sub, chans)
        return jax.shard_map(
            body,
            mesh=mesh,
            in_specs=(P(), P("win", "chan", None), P(), P()),
            out_specs=P("win", "chan", None, None, None),
            check_vma=False,
        )(table, traces, block_pairs, valid_count)

    return run
```

```python
import functools
import math

import jax
import jax.numpy as jnp
import ml_dtypes
import numpy as np
from jax import lax
from jax.experimental import pallas as pl
from jax.experimental.pallas import tpu as pltpu
from jax.sharding import PartitionSpec as P

BLOCK = 128
NBINS = 256
FREQ_LO = 64
GROUP = 32
GROUPS = NBINS // GROUP
EPS = 1e-06
MESH = pl.DeviceIdType.MESH
KCH = 4


def dft_table(length):
    times = np.arange(length, dtype=np.int32)
    freqs = FREQ_LO + np.arange(NBINS, dtype=np.int32)
    phases = times[:, None] * freqs[None, :] % length
    angles = phases.astype(np.float32) * np.float32(2.0 * math.pi / length)
    wide = angles.astype(np.float64)
    factor = np.float32(1.0 / math.sqrt(length))
    re = np.cos(wide).astype(np.float32) * factor
    im = -np.sin(wide).astype(np.float32) * factor
    table = np.stack(
        [re.reshape(length, GROUPS, GROUP), im.reshape(length, GROUPS, GROUP)], axis=2
    )
    return table.reshape(length, 2 * NBINS).astype(ml_dtypes.bfloat16)


def kernel(
    dims, tr_hbm, table_hbm, pairs, out,
    tr, table, acc, send, held, turned, held2, turned2, outbox, inbox, relay, value,
    in_sem, self_sem, a_send, a_recv, h_send, h_recv, p_send, p_recv, r_recv,
):
    planes, sub, chans, spp, spd, chl, length, relayed, forwards = dims
    win, x = lax.axis_index("win"), lax.axis_index("chan")
    q, j = win // sub, win % sub
    g = x * sub + j
    kc = length // KCH
    nch = chl // BLOCK
    both = jnp.logical_and
    last = planes - 1
    end = jnp.logical_or(q == 0, q == last)
    inner = jnp.logical_or(q == 1, q == last - 1)
    partner = jnp.where(q == 0, 1, jnp.where(q == 1, 0, jnp.where(q == last, last - 1, last)))
    by_data = (j % 2 == 0) if forwards else (j < 0)

    def tr_copy(c, k):
        part = (slice(None), pl.ds(c * BLOCK, BLOCK), pl.ds(k * kc, kc))
        return pltpu.make_async_copy(tr_hbm.at[part], tr.at[part], in_sem.at[c * KCH + k])

    def table_copy(k):
        part = pl.ds(k * kc, kc)
        return pltpu.make_async_copy(table_hbm.at[part], table.at[part], in_sem.at[nch * KCH + k])

    for k in range(KCH):
        tr_copy(0, k).start()
        table_copy(k).start()
    for c in range(1, nch):
        for k in range(KCH):
            tr_copy(c, k).start()

    barrier = pltpu.get_barrier_semaphore()

    @pl.loop(sub, GROUPS)
    def _(o):
        to = ((x * sub) + o) % GROUPS
        pl.semaphore_signal(
            barrier, inc=1, device_id=(q * sub + to % sub, to // sub), device_id_type=MESH
        )

    @pl.loop(1, planes * sub)
    def _(o):
        pl.semaphore_signal(
            barrier, inc=1, device_id=((win + o) % (planes * sub), x), device_id_type=MESH
        )

    def a_copy(c, o, to):
        return pltpu.make_async_remote_copy(
            src_ref=send.at[to, pl.ds(c * BLOCK, BLOCK), :],
            dst_ref=held.at[j, x * nch + c],
            send_sem=a_send.at[c, o],
            recv_sem=a_recv.at[c, o],
            device_id=(q * sub + to % sub, to // sub),
            device_id_type=MESH,
        )

    def h_copy(c, src):
        b = (src // sub) * nch + c
        return pltpu.make_async_remote_copy(
            src_ref=held.at[src % sub, b],
            dst_ref=held2.at[src % sub, b],
            send_sem=h_send.at[c, src],
            recv_sem=h_recv.at[c, src],
            device_id=(partner * sub + j, x),
            device_id_type=MESH,
        )

    def forward(c, src):
        if forwards:

            @pl.when(both(end, by_data))
            def _():
                h_copy(c, src).start()

    low = lax.broadcasted_iota(jnp.int32, (BLOCK, 128), 1) < 2 * GROUP
    for c in range(nch):
        for k in range(KCH):
            tr_copy(c, k).wait()
            if c == 0:
                table_copy(k).wait()
            rows = tr[:, c * BLOCK : (c + 1) * BLOCK, k * kc : (k + 1) * kc]
            term = jnp.dot(
                rows.reshape(2 * BLOCK, kc),
                table[k * kc : (k + 1) * kc, :],
                preferred_element_type=jnp.float32,
            )
            if k == 0:
                acc[...] = term
            else:
                acc[...] += term
        spectra = acc[...]
        energy = jnp.sum(spectra * spectra, axis=1, keepdims=True) / NBINS
        white = spectra * lax.rsqrt(energy + EPS)
        for h in range(GROUPS // 2):
            a = white[:BLOCK, h * 128 : (h + 1) * 128]
            b = white[BLOCK:, h * 128 : (h + 1) * 128]
            even = jnp.where(low, a, pltpu.roll(b, 64, 1))
            odd = jnp.where(low, pltpu.roll(a, 64, 1), b)
            send[2 * h, c * BLOCK : (c + 1) * BLOCK, :] = even.astype(jnp.bfloat16)
            send[2 * h + 1, c * BLOCK : (c + 1) * BLOCK, :] = odd.astype(jnp.bfloat16)
        if c == 0:
            pl.semaphore_wait(barrier, GROUPS - sub + planes * sub - 1)

        @pl.loop(1, GROUPS)
        def _(o):
            a_copy(c, o, (g + o) % GROUPS).start()

        pltpu.make_async_copy(
            send.at[g, pl.ds(c * BLOCK, BLOCK), :],
            held.at[j, x * nch + c],
            self_sem.at[c],
        ).start()

    for c in range(nch):
        pltpu.make_async_copy(
            send.at[g, pl.ds(c * BLOCK, BLOCK), :],
            held.at[j, x * nch + c],
            self_sem.at[c],
        ).wait()
        forward(c, g)

        @pl.loop(1, GROUPS)
        def _(o):
            src = (g + GROUPS - o) % GROUPS
            pltpu.make_async_remote_copy(
                src_ref=send.at[src, pl.ds(c * BLOCK, BLOCK), :],
                dst_ref=held.at[src % sub, (src // sub) * nch + c],
                send_sem=a_send.at[c, o],
                recv_sem=a_recv.at[c, o],
                device_id=(q * sub + src % sub, src // sub),
                device_id_type=MESH,
            ).wait_recv()
            forward(c, src)

    row = lax.broadcasted_iota(jnp.int32, (128, 128), 0)
    col = lax.broadcasted_iota(jnp.int32, (128, 128), 1)
    turn = jnp.where(
        col % (2 * GROUP) < GROUP,
        jnp.where(row == col + GROUP, 1.0, 0.0),
        jnp.where(row + GROUP == col, -1.0, 0.0),
    ).astype(jnp.bfloat16)

    def turn_all(held, turned):
        @pl.loop(0, chans * nch)
        def _(b):
            for m in range(sub):
                turned[m, b] = jnp.dot(
                    held[m, b], turn, preferred_element_type=jnp.float32
                ).astype(jnp.bfloat16)

    turn_all(held, turned)

    def partial(p, parts):
        r, s = pairs[0, p], pairs[1, p]
        upper = jnp.concatenate(
            [
                jnp.concatenate([have[m, r] for have, _ in parts for m in range(sub)], axis=1),
                jnp.concatenate([turn[m, r] for _, turn in parts for m in range(sub)], axis=1),
            ],
            axis=0,
        )
        lower = jnp.concatenate([have[m, s] for have, _ in parts for m in range(sub)], axis=1)
        return lax.dot_general(
            upper, lower, (((1,), (1,)), ((), ())), preferred_element_type=jnp.float32
        )

    def dest(k):
        return jnp.where(q < planes // 2, (q + planes - k) % planes, (q + k) % planes)

    def p_copy(d, i, t):
        return pltpu.make_async_remote_copy(
            src_ref=outbox.at[d, i],
            dst_ref=inbox.at[q, j, t % spd],
            send_sem=p_send.at[d, i],
            recv_sem=p_recv.at[q, j, t % spd],
            device_id=(d * sub + t // spd, x),
            device_id_type=MESH,
        )

    def r_copy(d, i):
        return pltpu.make_async_remote_copy(
            src_ref=outbox.at[d, i],
            dst_ref=relay.at[d, i],
            send_sem=p_send.at[d, i],
            recv_sem=r_recv.at[d, i],
            device_id=(partner * sub + j, x),
            device_id_type=MESH,
        )

    def item(n):
        k = n // spp
        if forwards:
            k = jnp.where(both(both(inner, by_data), k < last), (k + 1) % last, k)
        d, i = dest(k + 1), n % spp
        t = (j * spd + spd + i) % spp
        local = both(d == q, t // spd == j)
        return d, i, t, local

    @pl.loop(0, planes * spp)
    def _(n):
        d, i, t, local = item(n)
        if forwards:

            @pl.when(both(inner, both(by_data, n == 0)))
            def _():
                for c in range(nch):

                    @pl.loop(0, GROUPS)
                    def _(src):
                        h_copy(c, src).wait_recv()

                turn_all(held2, turned2)

        def work():
            own = [(held, turned)]
            if forwards:
                wide = both(inner, both(by_data, d != partner))

                @pl.when(wide)
                def _():
                    value[...] = partial(d * spp + t, own + [(held2, turned2)])

                @pl.when(jnp.logical_not(wide))
                def _():
                    value[...] = partial(d * spp + t, own)

            else:
                value[...] = partial(d * spp + t, own)

            if relayed:

                @pl.when(both(both(inner, jnp.logical_not(by_data)), both(d != partner, d != q)))
                def _():
                    r_copy(d, i).wait_recv()
                    value[...] += relay[d, i].astype(jnp.float32)

            @pl.when(local)
            def _():
                out[t % spd, j] = value[...]

            @pl.when(jnp.logical_not(local))
            def _():
                outbox[d, i] = value[...].astype(jnp.bfloat16)
                if relayed:
                    via = both(end, both(d != q, d != partner))

                    @pl.when(via)
                    def _():
                        r_copy(d, i).start()

                    @pl.when(jnp.logical_not(via))
                    def _():
                        p_copy(d, i, t).start()

                else:
                    p_copy(d, i, t).start()

        if forwards:
            pl.when(jnp.logical_not(both(both(end, by_data), d != q)))(work)
        else:
            work()

    def exists(src, m):
        there = jnp.logical_not(both(src == q, m == j))
        if relayed:
            src_end = jnp.logical_or(src == 0, src == last)
            src_partner = jnp.where(src == 0, 1, last - 1)
            direct = src_partner == q
            if forwards:
                direct = both(direct, m % 2 == 1)
            there = both(
                there, jnp.logical_or(src == q, jnp.logical_or(jnp.logical_not(src_end), direct))
            )
        return there

    @pl.loop(0, planes * sub)
    def _(n):
        src, m = (q + n // sub) % planes, n % sub

        @pl.when(exists(src, m))
        def _():
            for e in range(spd):
                pltpu.make_async_remote_copy(
                    src_ref=outbox.at[0, 0],
                    dst_ref=inbox.at[src, m, e],
                    send_sem=p_send.at[0, 0],
                    recv_sem=p_recv.at[src, m, e],
                    device_id=(src * sub + m, x),
                    device_id_type=MESH,
                ).wait_recv()
                got = inbox[src, m, e].astype(jnp.float32)

                @pl.when(both(n < sub, m != j))
                def _():
                    out[e, m] = got

                @pl.when(jnp.logical_not(both(n < sub, m != j)))
                def _():
                    out[e, m] += got

    for c in range(nch):

        @pl.loop(1, GROUPS)
        def _(o):
            a_copy(c, o, (g + o) % GROUPS).wait_send()

        if forwards:

            @pl.when(both(end, by_data))
            def _():
                @pl.loop(0, GROUPS)
                def _(src):
                    h_copy(c, src).wait_send()

    @pl.loop(0, planes * spp)
    def _(n):
        d, i, t, local = item(n)
        sent = jnp.logical_not(local)
        if forwards:
            sent = both(sent, jnp.logical_not(both(both(end, by_data), d != q)))

        @pl.when(sent)
        def _():
            p_copy(d, i, t).wait_send()


def on_device(planes, sub, chans, table, traces, block_pairs, valid_count):
    windows, chl, length = traces.shape
    slots = block_pairs.shape[0]
    spp, spd = slots // planes, slots // (planes * sub)
    relayed = planes >= 4
    dims = (planes, sub, chans, spp, spd, chl, length, relayed, relayed and sub > 1)
    bf, f32 = jnp.bfloat16, jnp.float32
    nch = chl // BLOCK
    sums = pl.pallas_call(
        functools.partial(kernel, dims),
        name="cross_spectra",
        out_shape=jax.ShapeDtypeStruct((spd, sub, 2 * BLOCK, BLOCK), f32),
        in_specs=[
            pl.BlockSpec(memory_space=pl.ANY),
            pl.BlockSpec(memory_space=pl.ANY),
            pl.BlockSpec(memory_space=pltpu.SMEM),
        ],
        out_specs=pl.BlockSpec(memory_space=pltpu.VMEM),
        scratch_shapes=[
            pltpu.VMEM((windows, chl, length), bf),
            pltpu.VMEM((length, 2 * NBINS), bf),
            pltpu.VMEM((windows * BLOCK, 2 * NBINS), f32),
            pltpu.VMEM((GROUPS, chl, 128), bf),
            pltpu.VMEM((sub, chans * nch, BLOCK, 128), bf),
            pltpu.VMEM((sub, chans * nch, BLOCK, 128), bf),
            pltpu.VMEM((sub, chans * nch, BLOCK, 128), bf),
            pltpu.VMEM((sub, chans * nch, BLOCK, 128), bf),
            pltpu.VMEM((planes, spp, 2 * BLOCK, BLOCK), bf),
            pltpu.VMEM((planes, sub, spd, 2 * BLOCK, BLOCK), bf),
            pltpu.VMEM((planes, spp, 2 * BLOCK, BLOCK), bf),
            pltpu.VMEM((2 * BLOCK, BLOCK), f32),
            pltpu.SemaphoreType.DMA(((nch + 1) * KCH,)),
            pltpu.SemaphoreType.DMA((nch,)),
            pltpu.SemaphoreType.DMA((nch, GROUPS)),
            pltpu.SemaphoreType.DMA((nch, GROUPS)),
            pltpu.SemaphoreType.DMA((nch, GROUPS)),
            pltpu.SemaphoreType.DMA((nch, GROUPS)),
            pltpu.SemaphoreType.DMA((planes, spp)),
            pltpu.SemaphoreType.DMA((planes, sub, spd)),
            pltpu.SemaphoreType.DMA((planes, spp)),
        ],
        compiler_params=pltpu.CompilerParams(
            collective_id=0, has_side_effects=True, vmem_limit_bytes=51 * 1024 * 1024
        ),
        cost_estimate=pl.CostEstimate(
            flops=2 * windows * chl * length * 2 * NBINS,
            bytes_accessed=2 * (windows * chl * length + length * 2 * NBINS),
            transcendentals=0,
        ),
    )(traces, table, block_pairs.T)
    stack_scale = 1.0 / math.sqrt(windows * planes * sub * GROUP)
    slot_ids = lax.axis_index("win") * spd + jnp.arange(spd, dtype=jnp.int32)
    live = (slot_ids < valid_count[0]).astype(f32)
    sums = sums.reshape(spd, sub, 2, BLOCK, BLOCK)
    return sums * (stack_scale * live)[:, None, None, None, None]


def solution(mesh):
    wins, chans = mesh.shape["win"], mesh.shape["chan"]
    sub = GROUPS // chans
    planes = wins // sub

    def run(traces, block_pairs, valid_count):
        table = jnp.asarray(dft_table(traces.shape[2]))
        body = functools.partial(on_device, planes, sub, chans)
        return jax.shard_map(
            body,
            mesh=mesh,
            in_specs=(P(), P("win", "chan", None), P(), P()),
            out_specs=P("win", "chan", None, None, None),
            check_vma=False,
        )(table, traces, block_pairs, valid_count)

    return run
```

```python
import functools
import math

import jax
import jax.numpy as jnp
import ml_dtypes
import numpy as np
from jax import lax
from jax.experimental import pallas as pl
from jax.experimental.pallas import tpu as pltpu
from jax.sharding import PartitionSpec as P

BLOCK = 128
NBINS = 256
FREQ_LO = 64
GROUP = 32
GROUPS = NBINS // GROUP
EPS = 1e-06
MESH = pl.DeviceIdType.MESH
KCH = 4


def dft_table(length):
    times = np.arange(length, dtype=np.int32)
    freqs = FREQ_LO + np.arange(NBINS, dtype=np.int32)
    phases = times[:, None] * freqs[None, :] % length
    angles = phases.astype(np.float32) * np.float32(2.0 * math.pi / length)
    wide = angles.astype(np.float64)
    factor = np.float32(1.0 / math.sqrt(length))
    re = np.cos(wide).astype(np.float32) * factor
    im = -np.sin(wide).astype(np.float32) * factor
    table = np.stack(
        [re.reshape(length, GROUPS, GROUP), im.reshape(length, GROUPS, GROUP)], axis=2
    )
    return table.reshape(length, 2 * NBINS).astype(ml_dtypes.bfloat16)


def kernel(
    dims, tr_hbm, table_hbm, pairs_hbm, out,
    tr, table, acc, send, held, turned, flipped, held2, turned2, flipped2, outbox, inbox, relay, value, pairs,
    in_sem, pairs_sem, self_sem, a_send, a_recv, h_send, h_recv, p_send, p_recv, r_recv,
):
    planes, sub, chans, spp, spd, chl, length, relayed, forwards = dims
    win, x = lax.axis_index("win"), lax.axis_index("chan")
    q, j = win // sub, win % sub
    g = x * sub + j
    kc = length // KCH
    nch = chl // BLOCK
    both = jnp.logical_and
    last = planes - 1
    end = jnp.logical_or(q == 0, q == last)
    inner = jnp.logical_or(q == 1, q == last - 1)
    partner = jnp.where(q == 0, 1, jnp.where(q == 1, 0, jnp.where(q == last, last - 1, last)))
    by_data = (j % 2 == 0) if forwards else (j < 0)

    def tr_copy(c, k):
        part = (slice(None), pl.ds(c * BLOCK, BLOCK), pl.ds(k * kc, kc))
        return pltpu.make_async_copy(tr_hbm.at[part], tr.at[part], in_sem.at[c * KCH + k])

    def table_copy(k):
        part = pl.ds(k * kc, kc)
        return pltpu.make_async_copy(table_hbm.at[part], table.at[part], in_sem.at[nch * KCH + k])

    for k in range(KCH):
        tr_copy(0, k).start()
        table_copy(k).start()
    for c in range(1, nch):
        for k in range(KCH):
            tr_copy(c, k).start()

    pairs_copy = pltpu.make_async_copy(pairs_hbm, pairs, pairs_sem)
    pairs_copy.start()

    barrier = pltpu.get_barrier_semaphore()

    @pl.loop(sub, GROUPS)
    def _(o):
        to = ((x * sub) + o) % GROUPS
        pl.semaphore_signal(
            barrier, inc=1, device_id=(q * sub + to % sub, to // sub), device_id_type=MESH
        )

    @pl.loop(1, planes * sub)
    def _(o):
        pl.semaphore_signal(
            barrier, inc=1, device_id=((win + o) % (planes * sub), x), device_id_type=MESH
        )

    def a_copy(c, o, to):
        return pltpu.make_async_remote_copy(
            src_ref=send.at[to, pl.ds(c * BLOCK, BLOCK), :],
            dst_ref=held.at[j, x * nch + c],
            send_sem=a_send.at[c, o],
            recv_sem=a_recv.at[c, o],
            device_id=(q * sub + to % sub, to // sub),
            device_id_type=MESH,
        )

    def h_copy(c, src):
        b = (src // sub) * nch + c
        return pltpu.make_async_remote_copy(
            src_ref=held.at[src % sub, b],
            dst_ref=held2.at[src % sub, b],
            send_sem=h_send.at[c, src],
            recv_sem=h_recv.at[c, src],
            device_id=(partner * sub + j, x),
            device_id_type=MESH,
        )

    def forward(c, src):
        if forwards:

            @pl.when(both(end, by_data))
            def _():
                h_copy(c, src).start()

    row = lax.broadcasted_iota(jnp.int32, (128, 128), 0)
    col = lax.broadcasted_iota(jnp.int32, (128, 128), 1)
    turn = jnp.where(
        col % (2 * GROUP) < GROUP,
        jnp.where(row == col + GROUP, 1.0, 0.0),
        jnp.where(row + GROUP == col, -1.0, 0.0),
    ).astype(jnp.bfloat16)
    eye = jnp.where(row == col, 1.0, 0.0).astype(jnp.bfloat16)

    def prepare(c, src, held, turned, flipped):
        m, b = src % sub, (src // sub) * nch + c
        piece = held[m, b]
        turned[m, b] = jnp.dot(piece, turn, preferred_element_type=jnp.float32).astype(
            jnp.bfloat16
        )
        flipped[m, b] = lax.dot_general(
            eye, piece, (((1,), (1,)), ((), ())), preferred_element_type=jnp.float32
        ).astype(jnp.bfloat16)

    low = lax.broadcasted_iota(jnp.int32, (BLOCK, 128), 1) < 2 * GROUP
    for c in range(nch):
        for k in range(KCH):
            tr_copy(c, k).wait()
            if c == 0:
                table_copy(k).wait()
            rows = tr[:, c * BLOCK : (c + 1) * BLOCK, k * kc : (k + 1) * kc]
            term = jnp.dot(
                rows.reshape(2 * BLOCK, kc),
                table[k * kc : (k + 1) * kc, :],
                preferred_element_type=jnp.float32,
            )
            if k == 0:
                acc[...] = term
            else:
                acc[...] += term
        spectra = acc[...]
        energy = jnp.sum(spectra * spectra, axis=1, keepdims=True) / NBINS
        white = spectra * lax.rsqrt(energy + EPS)
        for h in range(GROUPS // 2):
            a = white[:BLOCK, h * 128 : (h + 1) * 128]
            b = white[BLOCK:, h * 128 : (h + 1) * 128]
            even = jnp.where(low, a, pltpu.roll(b, 64, 1))
            odd = jnp.where(low, pltpu.roll(a, 64, 1), b)
            send[2 * h, c * BLOCK : (c + 1) * BLOCK, :] = even.astype(jnp.bfloat16)
            send[2 * h + 1, c * BLOCK : (c + 1) * BLOCK, :] = odd.astype(jnp.bfloat16)
        if c == 0:
            pl.semaphore_wait(barrier, GROUPS - sub + planes * sub - 1)

        @pl.loop(1, GROUPS)
        def _(o):
            a_copy(c, o, (g + o) % GROUPS).start()

        pltpu.make_async_copy(
            send.at[g, pl.ds(c * BLOCK, BLOCK), :],
            held.at[j, x * nch + c],
            self_sem.at[c],
        ).start()

    for c in range(nch):
        pltpu.make_async_copy(
            send.at[g, pl.ds(c * BLOCK, BLOCK), :],
            held.at[j, x * nch + c],
            self_sem.at[c],
        ).wait()
        forward(c, g)
        prepare(c, g, held, turned, flipped)

        @pl.loop(1, GROUPS)
        def _(o):
            src = (g + GROUPS - o) % GROUPS
            pltpu.make_async_remote_copy(
                src_ref=send.at[src, pl.ds(c * BLOCK, BLOCK), :],
                dst_ref=held.at[src % sub, (src // sub) * nch + c],
                send_sem=a_send.at[c, o],
                recv_sem=a_recv.at[c, o],
                device_id=(q * sub + src % sub, src // sub),
                device_id_type=MESH,
            ).wait_recv()
            forward(c, src)
            prepare(c, src, held, turned, flipped)

    def partial(p, parts):
        r, s = pairs[0, p], pairs[1, p]
        upper = jnp.concatenate(
            [
                jnp.concatenate([have[m, r] for have, _, _ in parts for m in range(sub)], axis=1),
                jnp.concatenate([rot[m, r] for _, rot, _ in parts for m in range(sub)], axis=1),
            ],
            axis=0,
        )
        lower = jnp.concatenate([flip[m, s] for _, _, flip in parts for m in range(sub)], axis=0)
        return jnp.dot(upper, lower, preferred_element_type=jnp.float32)

    def dest(k):
        return jnp.where(q < planes // 2, (q + planes - k) % planes, (q + k) % planes)

    def p_copy(d, i, t):
        return pltpu.make_async_remote_copy(
            src_ref=outbox.at[d, i],
            dst_ref=inbox.at[q, j, t % spd],
            send_sem=p_send.at[d, i],
            recv_sem=p_recv.at[q, j, t % spd],
            device_id=(d * sub + t // spd, x),
            device_id_type=MESH,
        )

    def r_copy(d, i):
        return pltpu.make_async_remote_copy(
            src_ref=outbox.at[d, i],
            dst_ref=relay.at[d, i],
            send_sem=p_send.at[d, i],
            recv_sem=r_recv.at[d, i],
            device_id=(partner * sub + j, x),
            device_id_type=MESH,
        )

    def item(n):
        k = n // spp
        if forwards:
            k = jnp.where(both(both(inner, by_data), k < last), (k + 1) % last, k)
        d, i = dest(k + 1), n % spp
        t = (j * spd + spd + i) % spp
        local = both(d == q, t // spd == j)
        return d, i, t, local

    pairs_copy.wait()

    @pl.loop(0, planes * spp)
    def _(n):
        d, i, t, local = item(n)
        if forwards:

            @pl.when(both(inner, both(by_data, n == 0)))
            def _():
                for c in range(nch):

                    @pl.loop(0, GROUPS)
                    def _(src):
                        h_copy(c, src).wait_recv()
                        prepare(c, src, held2, turned2, flipped2)


        def work():
            own = [(held, turned, flipped)]
            if forwards:
                wide = both(inner, both(by_data, d != partner))

                @pl.when(wide)
                def _():
                    value[...] = partial(d * spp + t, own + [(held2, turned2, flipped2)])

                @pl.when(jnp.logical_not(wide))
                def _():
                    value[...] = partial(d * spp + t, own)

            else:
                value[...] = partial(d * spp + t, own)

            if relayed:

                @pl.when(both(both(inner, jnp.logical_not(by_data)), both(d != partner, d != q)))
                def _():
                    r_copy(d, i).wait_recv()
                    value[...] += relay[d, i].astype(jnp.float32)

            @pl.when(local)
            def _():
                out[t % spd, j] = value[...]

            @pl.when(jnp.logical_not(local))
            def _():
                outbox[d, i] = value[...].astype(jnp.bfloat16)
                if relayed:
                    via = both(end, both(d != q, d != partner))

                    @pl.when(via)
                    def _():
                        r_copy(d, i).start()

                    @pl.when(jnp.logical_not(via))
                    def _():
                        p_copy(d, i, t).start()

                else:
                    p_copy(d, i, t).start()

        if forwards:
            pl.when(jnp.logical_not(both(both(end, by_data), d != q)))(work)
        else:
            work()

    def exists(src, m):
        there = jnp.logical_not(both(src == q, m == j))
        if relayed:
            src_end = jnp.logical_or(src == 0, src == last)
            src_partner = jnp.where(src == 0, 1, last - 1)
            direct = src_partner == q
            if forwards:
                direct = both(direct, m % 2 == 1)
            there = both(
                there, jnp.logical_or(src == q, jnp.logical_or(jnp.logical_not(src_end), direct))
            )
        return there

    @pl.loop(0, planes * sub)
    def _(n):
        src, m = (q + n // sub) % planes, n % sub

        @pl.when(exists(src, m))
        def _():
            for e in range(spd):
                pltpu.make_async_remote_copy(
                    src_ref=outbox.at[0, 0],
                    dst_ref=inbox.at[src, m, e],
                    send_sem=p_send.at[0, 0],
                    recv_sem=p_recv.at[src, m, e],
                    device_id=(src * sub + m, x),
                    device_id_type=MESH,
                ).wait_recv()
                got = inbox[src, m, e].astype(jnp.float32)

                @pl.when(both(n < sub, m != j))
                def _():
                    out[e, m] = got

                @pl.when(jnp.logical_not(both(n < sub, m != j)))
                def _():
                    out[e, m] += got

    for c in range(nch):

        @pl.loop(1, GROUPS)
        def _(o):
            a_copy(c, o, (g + o) % GROUPS).wait_send()

        if forwards:

            @pl.when(both(end, by_data))
            def _():
                @pl.loop(0, GROUPS)
                def _(src):
                    h_copy(c, src).wait_send()

    @pl.loop(0, planes * spp)
    def _(n):
        d, i, t, local = item(n)
        sent = jnp.logical_not(local)
        if forwards:
            sent = both(sent, jnp.logical_not(both(both(end, by_data), d != q)))

        @pl.when(sent)
        def _():
            p_copy(d, i, t).wait_send()


def on_device(planes, sub, chans, table, traces, block_pairs, valid_count):
    windows, chl, length = traces.shape
    slots = block_pairs.shape[0]
    spp, spd = slots // planes, slots // (planes * sub)
    relayed = planes >= 4
    dims = (planes, sub, chans, spp, spd, chl, length, relayed, relayed and sub > 1)
    bf, f32 = jnp.bfloat16, jnp.float32
    nch = chl // BLOCK
    sums = pl.pallas_call(
        functools.partial(kernel, dims),
        name="cross_spectra",
        out_shape=jax.ShapeDtypeStruct((spd, sub, 2 * BLOCK, BLOCK), f32),
        in_specs=[
            pl.BlockSpec(memory_space=pltpu.HBM),
            pl.BlockSpec(memory_space=pltpu.HBM),
            pl.BlockSpec(memory_space=pltpu.HBM),
        ],
        out_specs=pl.BlockSpec(memory_space=pltpu.VMEM),
        scratch_shapes=[
            pltpu.VMEM((windows, chl, length), bf),
            pltpu.VMEM((length, 2 * NBINS), bf),
            pltpu.VMEM((windows * BLOCK, 2 * NBINS), f32),
            pltpu.VMEM((GROUPS, chl, 128), bf),
            pltpu.VMEM((sub, chans * nch, BLOCK, 128), bf),
            pltpu.VMEM((sub, chans * nch, BLOCK, 128), bf),
            pltpu.VMEM((sub, chans * nch, BLOCK, 128), bf),
            pltpu.VMEM((sub, chans * nch, BLOCK, 128), bf),
            pltpu.VMEM((sub, chans * nch, BLOCK, 128), bf),
            pltpu.VMEM((sub, chans * nch, BLOCK, 128), bf),
            pltpu.VMEM((planes, spp, 2 * BLOCK, BLOCK), bf),
            pltpu.VMEM((planes, sub, spd, 2 * BLOCK, BLOCK), bf),
            pltpu.VMEM((planes, spp, 2 * BLOCK, BLOCK), bf),
            pltpu.VMEM((2 * BLOCK, BLOCK), f32),
            pltpu.SMEM((2, slots), jnp.int32),
            pltpu.SemaphoreType.DMA(((nch + 1) * KCH,)),
            pltpu.SemaphoreType.DMA,
            pltpu.SemaphoreType.DMA((nch,)),
            pltpu.SemaphoreType.DMA((nch, GROUPS)),
            pltpu.SemaphoreType.DMA((nch, GROUPS)),
            pltpu.SemaphoreType.DMA((nch, GROUPS)),
            pltpu.SemaphoreType.DMA((nch, GROUPS)),
            pltpu.SemaphoreType.DMA((planes, spp)),
            pltpu.SemaphoreType.DMA((planes, sub, spd)),
            pltpu.SemaphoreType.DMA((planes, spp)),
        ],
        compiler_params=pltpu.CompilerParams(
            collective_id=0, has_side_effects=True, vmem_limit_bytes=51 * 1024 * 1024
        ),
        cost_estimate=pl.CostEstimate(
            flops=2 * windows * chl * length * 2 * NBINS,
            bytes_accessed=2 * (windows * chl * length + length * 2 * NBINS),
            transcendentals=0,
        ),
    )(traces, table, block_pairs.T)
    stack_scale = 1.0 / math.sqrt(windows * planes * sub * GROUP)
    slot_ids = lax.axis_index("win") * spd + jnp.arange(spd, dtype=jnp.int32)
    live = (slot_ids < valid_count[0]).astype(f32)
    sums = sums.reshape(spd, sub, 2, BLOCK, BLOCK)
    return sums * (stack_scale * live)[:, None, None, None, None]


def solution(mesh):
    wins, chans = mesh.shape["win"], mesh.shape["chan"]
    sub = GROUPS // chans
    planes = wins // sub

    def run(traces, block_pairs, valid_count):
        table = jnp.asarray(dft_table(traces.shape[2]))
        body = functools.partial(on_device, planes, sub, chans)
        return jax.shard_map(
            body,
            mesh=mesh,
            in_specs=(P(), P("win", "chan", None), P(), P()),
            out_specs=P("win", "chan", None, None, None),
            check_vma=False,
        )(table, traces, block_pairs, valid_count)

    return run
```
